32 devices in a mesh: dp: 16 (over z, y, core), tensor: 2 (over x).
Axes of the slice: x: 2, y: 2, z: 4, core: 2. Of those that a mesh axis runs over, the one named last changes fastest.
Arguments:
- tokens: bfloat16 [2048, 2048], P('dp'), may hold values from -6 to 6
- cotangent: bfloat16 [2048, 2048], P('dp'), may hold values from -6 to 6
- lengths: int32 [16, 8], P('dp'), may hold values from 1 to 96, 128 in all within a row
- route: int32 [16, 128], P('dp'), may hold values from 0 to 127, each once within a row
- place: int32 [16, 128], P('dp'), may hold values from 0 to 127, each once within a row
- gain_one: bfloat16 [2048], P('dp'), may hold values from 0.5 to 1.5
- w_in: bfloat16 [2048, 2, 4096], P(None, None, ('dp', 'tensor')), may hold values from -0.125 to 0.125
- conv_w: bfloat16 [4, 4096], P(None, ('dp', 'tensor')), may hold values from -3 to 3
- conv_bias: bfloat16 [4096], P(('dp', 'tensor')), may hold values from -3 to 3
- w_x: bfloat16 [4096, 160], P(('dp', 'tensor')), may hold values from -0.09375 to 0.09375
- w_dt: bfloat16 [128, 4096], P(None, ('dp', 'tensor')), may hold values from -0.5 to 0.5
- dt_bias: bfloat16 [4096], P(('dp', 'tensor')), may hold values from -6 to -1
- a_log: bfloat16 [16, 4096], P(None, ('dp', 'tensor')), may hold values from -2 to 2.765625
- skip: bfloat16 [4096], P(('dp', 'tensor')), may hold values from 0.5 to 1.5
- w_out: bfloat16 [4096, 2048], P(('dp', 'tensor')), may hold values from -0.09375 to 0.09375
- gain_three: bfloat16 [2048], P('dp'), may hold values from 0.5 to 1.5
- mlp_one_in: bfloat16 [2048, 2, 8192], P('dp', None, 'tensor'), may hold values from -0.125 to 0.125
- mlp_one_out: bfloat16 [8192, 2048], P('tensor', 'dp'), may hold values from -0.0625 to 0.0625
- gain_two: bfloat16 [2048], P('dp'), may hold values from 0.5 to 1.5
- w_qkv: bfloat16 [2048, 3, 2048], P('dp', None, 'tensor'), may hold values from -0.125 to 0.125
- w_o: bfloat16 [2048, 2048], P('tensor', 'dp'), may hold values from -0.25 to 0.25
- gain_four: bfloat16 [2048], P('dp'), may hold values from 0.5 to 1.5
- mlp_two_in: bfloat16 [2048, 2, 8192], P('dp', None, 'tensor'), may hold values from -0.125 to 0.125
- mlp_two_out: bfloat16 [8192, 2048], P('tensor', 'dp'), may hold values from -0.0625 to 0.0625
Outputs:
- output: float32 [2048, 2048], P('dp')
- input_grad: float32 [2048, 2048], P('dp')
- grad_gain_one: float32 [2048], P('dp')
- grad_w_in: float32 [2048, 2, 4096], P(None, None, ('dp', 'tensor'))
- grad_conv_w: float32 [4, 4096], P(None, ('dp', 'tensor'))
- grad_conv_bias: float32 [4096], P(('dp', 'tensor'))
- grad_w_x: float32 [4096, 160], P(('dp', 'tensor'))
- grad_w_dt: float32 [128, 4096], P(None, ('dp', 'tensor'))
- grad_dt_bias: float32 [4096], P(('dp', 'tensor'))
- grad_a_log: float32 [16, 4096], P(None, ('dp', 'tensor'))
- grad_skip: float32 [4096], P(('dp', 'tensor'))
- grad_w_out: float32 [4096, 2048], P(('dp', 'tensor'))
- grad_gain_three: float32 [2048], P('dp')
- grad_mlp_one_in: float32 [2048, 2, 8192], P('dp', None, 'tensor')
- grad_mlp_one_out: float32 [8192, 2048], P('tensor', 'dp')
- grad_gain_two: float32 [2048], P('dp')
- grad_w_qkv: float32 [2048, 3, 2048], P('dp', None, 'tensor')
- grad_w_o: float32 [2048, 2048], P('tensor', 'dp')
- grad_gain_four: float32 [2048], P('dp')
- grad_mlp_two_in: float32 [2048, 2, 8192], P('dp', None, 'tensor')
- grad_mlp_two_out: float32 [8192, 2048], P('tensor', 'dp')
The draws below stay inside these ranges and needn't reach their ends.
Inputs may be any that keep to these rules, and one draw needn't show every extreme that they name: `route`: each device's row is a permutation of its local rows; entries k * 8 to k * 8 + 7 name the rows it sends to index k of dp. Each device's row is a permutation of the rows it receives, numbered by sending index of dp and then by their place in the sender's slot. Each device's 8 lengths sum to 128.
All inputs are finite; a program needn't handle non-finite values.
Results may differ from the reference program's by a relative error of at most 0.02.
Values may be sent and summed in bfloat16 or wider, within the bound.
No kernel may reach another device: no remote copies, remote signals or barrier semaphores. Data moves between devices by JAX's collectives and lax.ppermute only.
A program may use at most 512 MiB of HBM per device.

```python
import math
import jax
import jax.numpy as jnp
import numpy as np
from jax import lax

D = 2048
E = 4096
N = 16
R = 128
K = 4
H = 32
HD = 64
FF = 8192
TOK_DEV = 128
SEQS = 8
BLOCK = 16
MAXLEN = 96
TOKENS = 2048
N_DP = 16


def block_levels(own_key, shape, shards, least, largest):
    gain, own = 1.0, jax.random.fold_in(own_key, 6)
    for axis_at, shards_of in shards:
        heights = jnp.exp(jax.random.uniform(jax.random.fold_in(own, axis_at), (shards_of,), jnp.float32, least / len(shards), largest / len(shards)))
        gain = gain * jnp.repeat(heights, shape[axis_at] // shards_of).reshape([-1 if axis == axis_at else 1 for axis in range(len(shape))])
    return gain


def split_up(number_of, total, bound, lean):
    weights = [(1 << 20) // math.isqrt(standing ** lean) + 1 for standing in range(2, number_of + 1)]
    rest, counts = total - bound - (number_of - 1), [1] * (number_of - 1)
    while rest > 0:
        movable = [i for i in range(number_of - 1) if counts[i] < bound]
        mass, left = sum([weights[i] for i in movable]), rest
        for i in movable:
            addition = min(bound - counts[i], max(1, left * weights[i] // mass), rest)
            counts[i] = counts[i] + addition
            rest = rest - addition
    return np.array([bound] + counts)


def uneven_parts(stream_key, number_of, total, reach, slope):
    if number_of == 2:
        one = jax.random.randint(stream_key, (), max(1, total - reach), min(reach, total - 1) + 1)
        return jnp.stack([one, total - one])
    tallies = jnp.asarray(split_up(number_of, total, reach, slope), jnp.int32)
    pairs = (number_of - 1) // 2
    source_of, sink = tallies[1:1 + 2 * pairs:2], tallies[2:2 + 2 * pairs:2]
    room = jnp.minimum(source_of - 1, reach - sink)
    shifted = jax.random.randint(jax.random.fold_in(stream_key, 1), (pairs,), 0, 1 << 20) % (room + 1)
    tallies = tallies.at[1:1 + 2 * pairs:2].set(source_of - shifted).at[2:2 + 2 * pairs:2].set(sink + shifted)
    return tallies[jax.random.permutation(jax.random.fold_in(stream_key, 2), number_of)]


def centred(rng, dims, deviation, reach, pieces=(), kind=jnp.bfloat16):
    values = deviation * jax.random.normal(rng, dims, jnp.float32)
    if pieces:
        values = values * block_levels(rng, dims, pieces, -0.22, 0.18)
    return jnp.clip(values, -reach, reach).astype(kind)


def setup_inputs(seed: int = 0) -> dict:
    splits = jax.random.split(jax.random.key(seed), 25)
    return {
        "tokens": centred(splits[0], (TOKENS, D), 1.0, 6.0, ((0, 16),)),
        "cotangent": centred(splits[1], (TOKENS, D), 1.0, 6.0, ((0, 16),)),
        "lengths": jax.vmap(lambda own: uneven_parts(own, SEQS, TOK_DEV, MAXLEN, 2))(jax.random.split(splits[2], N_DP)).reshape((N_DP, SEQS)).astype(jnp.int32),
        "route": jax.vmap(lambda own: jax.random.permutation(own, TOK_DEV))(jax.random.split(splits[3], N_DP)).reshape((N_DP, TOK_DEV)).astype(jnp.int32),
        "place": jax.vmap(lambda own: jax.random.permutation(own, TOK_DEV))(jax.random.split(splits[4], N_DP)).reshape((N_DP, TOK_DEV)).astype(jnp.int32),
        "gain_one": jnp.clip(1.0 + 0.1 * jax.random.normal(splits[5], (D,), jnp.float32), 0.5, 1.5).astype(jnp.bfloat16),
        "w_in": centred(splits[6], (D, 2, E), D ** -0.5, 0.125, ((2, 32),)),
        "conv_w": centred(splits[7], (K, E), K ** -0.5, 3.0, ((1, 32),)),
        "conv_bias": centred(splits[8], (E,), 0.5, 3.0, ((0, 32),)),
        "w_x": centred(splits[9], (E, R + 2 * N), E ** -0.5, 0.09375, ((0, 32),)),
        "w_dt": centred(splits[10], (R, E), R ** -0.5, 0.5, ((1, 32),)),
        "dt_bias": jnp.clip(-6.0 + 5.0 * jax.random.uniform(splits[11], (E,), jnp.float32) ** block_levels(splits[11], (E,), ((0, 32),), -0.2, 0.2), -6.0, -1.0).astype(jnp.bfloat16),
        "a_log": jnp.clip(-2.0 + 4.765625 * jax.random.uniform(splits[12], (N, E), jnp.float32) ** block_levels(splits[12], (N, E), ((1, 32),), -0.2, 0.2), -2.0, 2.765625).astype(jnp.bfloat16),
        "skip": jnp.clip(0.5 + 1.0 * jax.random.uniform(splits[13], (E,), jnp.float32) ** block_levels(splits[13], (E,), ((0, 32),), -0.2, 0.2), 0.5, 1.5).astype(jnp.bfloat16),
        "w_out": centred(splits[14], (E, D), E ** -0.5, 0.09375, ((0, 32),)),
        "gain_three": jnp.clip(1.0 + 0.1 * jax.random.normal(splits[15], (D,), jnp.float32), 0.5, 1.5).astype(jnp.bfloat16),
        "mlp_one_in": centred(splits[16], (D, 2, FF), D ** -0.5, 0.125, ((0, 16), (2, 2))),
        "mlp_one_out": centred(splits[17], (FF, D), FF ** -0.5, 0.0625, ((0, 2), (1, 16))),
        "gain_two": jnp.clip(1.0 + 0.1 * jax.random.normal(splits[18], (D,), jnp.float32), 0.5, 1.5).astype(jnp.bfloat16),
        "w_qkv": centred(splits[19], (D, 3, H * HD), D ** -0.5, 0.125, ((0, 16), (2, 2))),
        "w_o": centred(splits[20], (H * HD, D), (D // 4) ** -0.5, 0.25, ((0, 2), (1, 16))),
        "gain_four": jnp.clip(1.0 + 0.1 * jax.random.normal(splits[21], (D,), jnp.float32), 0.5, 1.5).astype(jnp.bfloat16),
        "mlp_two_in": centred(splits[22], (D, 2, FF), D ** -0.5, 0.125, ((0, 16), (2, 2))),
        "mlp_two_out": centred(splits[23], (FF, D), FF ** -0.5, 0.0625, ((0, 2), (1, 16))),
    }


eps = 1e-05
precise = lax.Precision.HIGHEST

@jax.custom_vjp
def low(v):
    return lax.optimization_barrier(v.astype(jnp.bfloat16)).astype(jnp.float32)

@jax.custom_vjp
def low_back(v):
    return v

def low_keep(v):
    return (low(v), None)

def low_pass(kept, grad):
    return (grad,)

def back_keep(v):
    return (v, None)

def back_low(kept, grad):
    return (low(grad),)
low.defvjp(low_keep, low_pass)
low_back.defvjp(back_keep, back_low)

def matmul(left_side, right_side):
    return jnp.dot(left_side, right_side, precision=precise)

def seq_layout(lens_row):
    seq_ends = jnp.cumsum(lens_row)
    begins = seq_ends - lens_row
    row_index = jnp.arange(TOK_DEV, dtype=jnp.int32)
    segment = lax.optimization_barrier(jnp.sum((row_index[:, None] >= seq_ends[None, :]).astype(jnp.int32), axis=1))
    one_hot = (segment[:, None] == jnp.arange(lens_row.shape[0], dtype=jnp.int32)[None, :]).astype(jnp.int32)
    return (segment, row_index - lax.optimization_barrier(jnp.sum(one_hot * begins[None, :], axis=1)))

def rms_normed(stream, gain_vec):
    return stream * lax.rsqrt(lax.optimization_barrier(jnp.mean(stream * stream, axis=-1, keepdims=True)) + eps) * gain_vec[None, :]

def rotated(heads_in, cosine, sine_part):
    half_width = heads_in.shape[-1] // 2
    first_half = heads_in[..., :half_width]
    second_half = heads_in[..., half_width:]
    return jnp.concatenate([first_half * cosine - second_half * sine_part, second_half * cosine + first_half * sine_part], axis=-1)

def combine(earlier, latter):
    return (earlier[0] * latter[0], latter[0] * earlier[1] + latter[1])

def selective_scan(stepsize, mixer_val, input_mat, output_mat, keep_mask, decay_rate):
    block_count = stepsize.shape[0] // BLOCK

    def blocked(values):
        return values.reshape((block_count, BLOCK) + values.shape[1:])

    @jax.checkpoint
    def block_step(state_now, slices):
        step_now, mixer_now, input_now, output_now, keep_now = slices
        decays = jnp.exp(step_now[:, None, :] * decay_rate[None]) * keep_now[:, None, None]
        source = (step_now * mixer_now)[:, None, :] * input_now[:, :, None]
        factors, partial_sums = lax.associative_scan(combine, (decays, source), axis=0)
        states = factors * state_now[None] + partial_sums
        return (states[-1], lax.optimization_barrier(jnp.sum(output_now[:, :, None] * states, axis=1)))
    initial = jnp.zeros(decay_rate.shape, stepsize.dtype)
    unused, outputs = lax.scan(block_step, initial, (blocked(stepsize), blocked(mixer_val), blocked(input_mat), blocked(output_mat), blocked(keep_mask)))
    return outputs.reshape(stepsize.shape)

def feed_forward(stream, gain_vec, gate_up, down_proj):
    normed = low(rms_normed(stream, gain_vec))
    pair = low_back(jnp.einsum('td,dcf->tcf', normed, gate_up, precision=precise))
    hidden = low(jax.nn.silu(pair[:, 0]) * pair[:, 1])
    return stream + low_back(matmul(hidden, down_proj))

def layer(stream, lens_row, params):
    gain_one, w_in, conv_w, conv_bias, w_x, w_dt, dt_bias, a_log, skip, w_out, gain_three, mlp_one_in, mlp_one_out, gain_two, w_qkv, w_o, gain_four, mlp_two_in, mlp_two_out = params
    segment, offset = seq_layout(lens_row)
    keep_mask = (offset > 0).astype(stream.dtype)
    normed_one = low(rms_normed(stream, gain_one))
    inner_pair = low_back(jnp.einsum('td,dce->tce', normed_one, w_in, precision=precise))
    conv_input = inner_pair[:, 0]
    gate_input = inner_pair[:, 1]
    conv_sum = conv_bias[None, :] + conv_w[0][None, :] * conv_input
    for tap_index in range(1, K):
        delayed_in = jnp.concatenate([jnp.zeros((tap_index, conv_input.shape[1]), conv_input.dtype), conv_input[:-tap_index]], axis=0)
        conv_sum = conv_sum + conv_w[tap_index][None, :] * delayed_in * (offset >= tap_index).astype(stream.dtype)[:, None]
    mixer_low = low(jax.nn.silu(conv_sum))
    selected = low_back(matmul(mixer_low, w_x))
    step_low = low(selected[:, :R])
    stepsize = jax.nn.softplus(low_back(matmul(step_low, w_dt) + dt_bias[None, :]))
    decay_rate = -jnp.exp(a_log)
    scanned = selective_scan(stepsize, mixer_low, selected[:, R:R + N], selected[:, R + N:], keep_mask, decay_rate)
    mixer_out = scanned + skip[None, :] * mixer_low
    gated_low = low(mixer_out * jax.nn.silu(gate_input))
    stream_mid = stream + low_back(matmul(gated_low, w_out))
    stream_ffn = feed_forward(stream_mid, gain_three, mlp_one_in, mlp_one_out)
    normed_two = low(rms_normed(stream_ffn, gain_two))
    row_count = stream.shape[0]
    head_count = w_qkv.shape[2] // HD
    projected = low_back(jnp.einsum('td,dcf->tcf', normed_two, w_qkv, precision=precise)).reshape(row_count, 3, head_count, HD)
    half_width = HD // 2
    inverse = 10000.0 ** (-jnp.arange(half_width).astype(stream.dtype) / half_width)
    angle_table = offset.astype(stream.dtype)[:, None] * inverse[None, :]
    cosine = jnp.cos(angle_table)[:, None, :]
    sine_part = jnp.sin(angle_table)[:, None, :]
    query_low = low(rotated(projected[:, 0], cosine, sine_part) * HD ** (-0.5))
    key_low = low(rotated(projected[:, 1], cosine, sine_part))
    value_low = low(projected[:, 2])
    scores = low_back(jnp.einsum('thd,shd->hts', query_low, key_low, precision=precise))
    row_index = jnp.arange(row_count)
    allowed = (segment[:, None] == segment[None, :]) & (row_index[:, None] >= row_index[None, :])
    attn_probs = jax.nn.softmax(jnp.where(allowed[None], scores, -1e+30), axis=-1)
    context = low(low_back(jnp.einsum('hts,shd->thd', low(attn_probs), value_low, precision=precise)))
    stream_attn = stream_ffn + low_back(matmul(context.reshape(row_count, head_count * HD), w_o))
    return feed_forward(stream_attn, gain_four, mlp_two_in, mlp_two_out)

def reference(tokens, cotangent, lengths, route, place, gain_one, w_in, conv_w, conv_bias, w_x, w_dt, dt_bias, a_log, skip, w_out, gain_three, mlp_one_in, mlp_one_out, gain_two, w_qkv, w_o, gain_four, mlp_two_in, mlp_two_out):
    dev_count = route.shape[0]
    slot_rows = TOK_DEV // dev_count
    target = jnp.arange(dev_count, dtype=jnp.int32)[:, None]
    source_dev = (place // slot_rows).astype(jnp.int32)
    sent_row = (target * slot_rows + place % slot_rows).astype(jnp.int32)
    home_rows = (source_dev * TOK_DEV + route[source_dev, sent_row]).astype(jnp.int32).reshape(-1)
    model_width = tokens.shape[1]
    params = tuple([weight.astype(jnp.float32) for weight in (gain_one, w_in, conv_w, conv_bias, w_x, w_dt, dt_bias, a_log, skip, w_out, gain_three, mlp_one_in, mlp_one_out, gain_two, w_qkv, w_o, gain_four, mlp_two_in, mlp_two_out)])

    def forward(stream, weights_in):
        packed = stream[home_rows].reshape(dev_count, TOK_DEV, model_width)

        def one_device(device_pair):
            return layer(device_pair[0], device_pair[1], weights_in)
        outputs = lax.map(jax.checkpoint(one_device), (packed, lengths))
        return jnp.zeros_like(stream).at[home_rows].set(outputs.reshape(-1, model_width))
    output, pullback = jax.vjp(forward, tokens.astype(jnp.float32), params)
    input_grad, weight_grads = pullback(cotangent.astype(jnp.float32))
    return (output, input_grad, weight_grads[0], weight_grads[1], weight_grads[2], weight_grads[3], weight_grads[4], weight_grads[5], weight_grads[6], weight_grads[7], weight_grads[8], weight_grads[9], weight_grads[10], weight_grads[11], weight_grads[12], weight_grads[13], weight_grads[14], weight_grads[15], weight_grads[16], weight_grads[17], weight_grads[18])
```

```python
import functools

import jax
import jax.numpy as jnp
from jax import lax
from jax.experimental import pallas as pl
from jax.experimental.pallas import tpu as pltpu
from jax.sharding import PartitionSpec as P

N = 16
R = 128
K = 4
HD = 64
LANE = 128
GROUP = 8
LOG2E = 1.4426950408889634
LN2 = 0.6931471805599453

low = jnp.bfloat16
full = jnp.float32
eps = 1e-05


def block_rows(ref, start, count, stride):
    return ref[pl.ds(start, count, stride=stride), :]


def spread(ref, values):
    rows = values.shape[0]
    for part in range(values.shape[1] // LANE):
        ref[part * rows : (part + 1) * rows, :] = values[:, part * LANE : (part + 1) * LANE]


def gathered(ref, rows):
    return jnp.concatenate(
        [ref[part * rows : (part + 1) * rows, :] for part in range(ref.shape[0] // rows)], axis=1
    )


def scan_forward_kernel(
    packs, chunk, mixer_ref, gate_ref, low_ref, mats_ref, keep_ref, proj_ref, bias_ref, rate_ref, skip_ref,
    gated_ref, out_ref, prior_ref, step_s, drive_s, out_s, rate_s, state,
):
    rows, width = mixer_ref.shape
    span = rows // packs
    parts = width // LANE
    place = pl.program_id(0)

    @pl.when(place == 0)
    def _():
        state[...] = jnp.zeros_like(state)
        pre = jnp.dot(low_ref[...], proj_ref[...], preferred_element_type=jnp.float32) + bias_ref[...]
        step = jax.nn.softplus(pre)
        spread(drive_s, step * mixer_ref[...])
        spread(step_s, jnp.where(keep_ref[...] > 0.0, step, 1e30))
        for n in range(N):
            for part in range(parts):
                rate_s[n, part] = jnp.broadcast_to(
                    rate_ref[n : n + 1, part * LANE : (part + 1) * LANE] * LOG2E, (packs, LANE)
                )

    def one(k, held):
        t = place * chunk + k
        mats = block_rows(mats_ref, t, packs, span)
        step_now = [block_rows(step_s, part * rows + t, packs, span) for part in range(parts)]
        drive_now = [block_rows(drive_s, part * rows + t, packs, span) for part in range(parts)]
        total = [jnp.zeros((packs, LANE), jnp.float32)] * parts
        fresh = []
        for n in range(N):
            source = jnp.broadcast_to(mats[:, n : n + 1], (packs, LANE))
            reader = jnp.broadcast_to(mats[:, N + n : N + n + 1], (packs, LANE))
            for part in range(parts):
                before = held[n * parts + part]
                prior_ref[k, n, part] = before
                now = jnp.exp2(step_now[part] * rate_s[n, part]) * before + drive_now[part] * source
                total[part] = total[part] + reader * now
                fresh.append(now)
        for part in range(parts):
            out_s[pl.ds(part * rows + t, packs, stride=span), :] = total[part]
        return tuple(fresh)

    final = lax.fori_loop(
        0, chunk, one, tuple(state[n, part] for n in range(N) for part in range(parts))
    )
    for n in range(N):
        for part in range(parts):
            state[n, part] = final[n * parts + part]

    @pl.when(place == pl.num_programs(0) - 1)
    def _():
        mixed = gathered(out_s, rows) + skip_ref[...] * mixer_ref[...]
        out_ref[...] = mixed
        gate = gate_ref[...]
        gated_ref[...] = (mixed * gate * jax.nn.sigmoid(gate)).astype(jnp.bfloat16)


def whole_block(shape):
    return pl.BlockSpec(shape, lambda c: (0,) * len(shape))


def scan_forward(mixer, gate, low, mats, keep, proj, bias, rate, skip, packs, chunk=16):
    rows, width = mixer.shape
    span = rows // packs
    parts = width // LANE
    args = (mixer, gate, low, mats, keep, proj, bias, rate, skip)
    return pl.pallas_call(
        functools.partial(scan_forward_kernel, packs, chunk),
        grid=(span // chunk,),
        in_specs=[whole_block(value.shape) for value in args],
        out_specs=[
            whole_block((rows, width)),
            whole_block((rows, width)),
            pl.BlockSpec((chunk, N, parts, packs, LANE), lambda c: (c, 0, 0, 0, 0)),
        ],
        out_shape=[
            jax.ShapeDtypeStruct((rows, width), jnp.bfloat16),
            jax.ShapeDtypeStruct((rows, width), jnp.float32),
            jax.ShapeDtypeStruct((span, N, parts, packs, LANE), jnp.float32),
        ],
        scratch_shapes=[
            pltpu.VMEM((parts * rows, LANE), jnp.float32),
            pltpu.VMEM((parts * rows, LANE), jnp.float32),
            pltpu.VMEM((parts * rows, LANE), jnp.float32),
            pltpu.VMEM((N, parts, packs, LANE), jnp.float32),
            pltpu.VMEM((N, parts, packs, LANE), jnp.float32),
        ],
        compiler_params=pltpu.CompilerParams(vmem_limit_bytes=48 << 20),
        cost_estimate=pl.CostEstimate(
            flops=rows * width * N * 8, bytes_accessed=rows * width * N * 4, transcendentals=rows * width * N
        ),
    )(*args)


def scan_backward_kernel(
    packs, chunk, mixer_ref, gate_ref, mixed_ref, gated_ref, low_ref, mats_ref, keep_ref, proj_ref, bias_ref,
    rate_ref, skip_ref, prior_ref,
    step_grad_ref, mixer_grad_ref, gate_grad_ref, mats_grad_ref, log_grad_ref, skip_grad_ref,
    step_s, drive_s, mix_s, grad_s, rate_s, total_s, along_s, log_s, state,
):
    rows, width = mixer_ref.shape
    span = rows // packs
    parts = width // LANE
    place = pl.program_id(0)
    lane = lax.broadcasted_iota(jnp.int32, (packs, LANE), 1)

    def step_before():
        return (
            jnp.dot(low_ref[...], proj_ref[...], preferred_element_type=jnp.float32) + bias_ref[...]
        )

    @pl.when(place == 0)
    def _():
        state[...] = jnp.zeros_like(state)
        log_s[...] = jnp.zeros_like(log_s)
        step = jax.nn.softplus(step_before())
        mixer = mixer_ref[...]
        gate = gate_ref[...]
        sig = jax.nn.sigmoid(gate)
        grad = gated_ref[...]
        scan_grad = grad * gate * sig
        gate_grad_ref[...] = (grad * mixed_ref[...] * sig * (1.0 + gate * (1.0 - sig))).astype(jnp.bfloat16)
        skip_grad_ref[...] = jnp.sum(scan_grad * mixer, axis=0, keepdims=True)
        spread(grad_s, scan_grad)
        spread(mix_s, mixer)
        spread(drive_s, step * mixer)
        spread(step_s, jnp.where(keep_ref[...] > 0.0, step, 1e30))
        for n in range(N):
            for part in range(parts):
                rate_s[n, part] = jnp.broadcast_to(
                    rate_ref[n : n + 1, part * LANE : (part + 1) * LANE] * LOG2E, (packs, LANE)
                )

    def one(back, held):
        k = chunk - 1 - back
        t = (pl.num_programs(0) - 1 - place) * chunk + k
        mats = block_rows(mats_ref, t, packs, span)
        step_now = [block_rows(step_s, part * rows + t, packs, span) for part in range(parts)]
        drive_now = [block_rows(drive_s, part * rows + t, packs, span) for part in range(parts)]
        mix_now = [block_rows(mix_s, part * rows + t, packs, span) for part in range(parts)]
        grad_now = [block_rows(grad_s, part * rows + t, packs, span) for part in range(parts)]
        zero = jnp.zeros((packs, LANE), jnp.float32)
        along = [zero] * parts
        rated = [zero] * parts
        waiting = []
        fresh = []
        for n in range(N):
            source = jnp.broadcast_to(mats[:, n : n + 1], (packs, LANE))
            reader = jnp.broadcast_to(mats[:, N + n : N + n + 1], (packs, LANE))
            source_sum = zero
            reader_sum = zero
            for part in range(parts):
                rate = rate_s[n, part]
                decay = jnp.exp2(step_now[part] * rate)
                kept = decay * prior_ref[k, n, part]
                now = kept + drive_now[part] * source
                adjoint = grad_now[part] * reader + held[n * parts + part]
                fresh.append(decay * adjoint)
                through = adjoint * kept
                rated[part] = rated[part] + through * rate
                log_s[n, part] += through * step_now[part]
                along[part] = along[part] + adjoint * source
                source_sum = source_sum + adjoint * drive_now[part]
                reader_sum = reader_sum + grad_now[part] * now
            waiting.append(source_sum)
            waiting.append(reader_sum)
        for part in range(parts):
            total_s[pl.ds(part * rows + t, packs, stride=span), :] = rated[part] * LN2 + mix_now[part] * along[part]
            along_s[pl.ds(part * rows + t, packs, stride=span), :] = along[part]
        big = jnp.dot(jnp.concatenate(waiting, axis=0).astype(jnp.bfloat16), jnp.ones((LANE, LANE), jnp.bfloat16), preferred_element_type=jnp.float32)
        mats_grad = zero
        for q in range(2 * N):
            mats_grad = jnp.where(lane == q, big[q * packs : (q + 1) * packs], mats_grad)
        mats_grad_ref[pl.ds(t, packs, stride=span), :] = mats_grad
        return tuple(fresh)

    final = lax.fori_loop(
        0, chunk, one, tuple(state[n, part] for n in range(N) for part in range(parts))
    )
    for n in range(N):
        for part in range(parts):
            state[n, part] = final[n * parts + part]

    @pl.when(place == pl.num_programs(0) - 1)
    def _():
        pre = step_before()
        step_grad_ref[...] = (gathered(total_s, rows) * jax.nn.sigmoid(pre)).astype(jnp.bfloat16)
        mixer_grad_ref[...] = (
            gathered(along_s, rows) * jax.nn.softplus(pre) + skip_ref[...] * gathered(grad_s, rows)
        )
        for n in range(N):
            log_grad_ref[n : n + 1, :] = jnp.concatenate(
                [jnp.sum(log_s[n, part], axis=0, keepdims=True) for part in range(parts)], axis=1
            ) * rate_ref[n : n + 1, :]


def scan_backward(
    mixer, gate, mixed, gated_grad, low, mats, keep, proj, bias, rate, skip, prior, packs, chunk=16
):
    rows, width = mixer.shape
    span = rows // packs
    parts = width // LANE
    last = span // chunk - 1
    args = (mixer, gate, mixed, gated_grad, low, mats, keep, proj, bias, rate, skip)
    shapes = [
        ((rows, width), jnp.bfloat16),
        ((rows, width), jnp.float32),
        ((rows, width), jnp.bfloat16),
        ((rows, LANE), jnp.float32),
        ((N, width), jnp.float32),
        ((1, width), jnp.float32),
    ]
    long_row = pltpu.VMEM((parts * rows, LANE), jnp.float32)
    small = pltpu.VMEM((N, parts, packs, LANE), jnp.float32)
    return pl.pallas_call(
        functools.partial(scan_backward_kernel, packs, chunk),
        grid=(span // chunk,),
        in_specs=[whole_block(value.shape) for value in args]
        + [pl.BlockSpec((chunk, N, parts, packs, LANE), lambda c: (last - c, 0, 0, 0, 0))],
        out_specs=[whole_block(shape) for shape, kind in shapes],
        out_shape=[jax.ShapeDtypeStruct(shape, kind) for shape, kind in shapes],
        scratch_shapes=[long_row, long_row, long_row, long_row, small, long_row, long_row, small, small],
        compiler_params=pltpu.CompilerParams(vmem_limit_bytes=56 << 20),
        cost_estimate=pl.CostEstimate(
            flops=rows * width * N * 20, bytes_accessed=rows * width * N * 4, transcendentals=rows * width * N
        ),
    )(*args, prior)


def silu_slope(operand):
    sig_value = jax.nn.sigmoid(operand)
    return sig_value * (1.0 + operand * (1.0 - sig_value))


def matmul(left, right):
    return jnp.dot(left, right, preferred_element_type=full)


def matmul_rows(left, right):
    return lax.dot_general(left, right, (((0,), (0,)), ((), ())), preferred_element_type=full)


def matmul_lanes(left, right):
    return lax.dot_general(left, right, (((1,), (1,)), ((), ())), preferred_element_type=full)


def norm_scale(stream):
    return lax.rsqrt(jnp.mean(stream * stream, axis=-1, keepdims=True) + eps)


def normed_rows(stream, gain):
    scale = norm_scale(stream)
    return scale, (stream * scale * gain[None, :]).astype(low)


def norm_backward(stream, rms_scale, gain_vec, grad_normed):
    weighted = grad_normed * gain_vec[None, :]
    inner_mean = jnp.mean(weighted * stream, axis=-1, keepdims=True)
    grad_stream = rms_scale * weighted - stream * rms_scale * rms_scale * rms_scale * inner_mean
    return (grad_stream, jnp.sum(grad_normed * stream * rms_scale, axis=0))


def hop(values, link):
    if link == "x":
        return lax.ppermute(values, "tensor", [(0, 1), (1, 0)])
    bit = {"core": 1, "y": 2, "z": 4, "outer": GROUP}[link]
    return lax.ppermute(values, "dp", [(k, k ^ bit) for k in range(lax.axis_size("dp"))])


def ordered(mine, theirs, index):
    first = index == 0
    return jnp.where(first, mine, theirs), jnp.where(first, theirs, mine)


def cuts(rows):
    third = rows * 3 // 8
    return ((0, third), (third, 2 * third), (2 * third, rows))


def gather_rows(own):
    tensor_at = lax.axis_index("tensor")

    def grow(values, axis, link):
        got = hop(values, link)
        if link == "x":
            return jnp.stack(ordered(values, got, tensor_at), axis=axis)
        return jnp.stack([values, got], axis=axis)

    first, second, third = [own[start:stop] for start, stop in cuts(own.shape[0])]
    first = grow(grow(grow(first, 0, "x"), 0, "y"), 0, "z")
    second = grow(grow(grow(second, 0, "y"), 0, "z"), 2, "x")
    third = grow(grow(grow(third, 0, "z"), 1, "x"), 1, "y")
    local = jnp.concatenate([first, second, third], axis=3)
    both = jnp.stack([local, hop(local, "core")], axis=0)
    return both.reshape((2 * GROUP * own.shape[0], own.shape[1]))


def reduce_rows(partial):
    kind = partial.dtype
    tensor_at = lax.axis_index("tensor")
    width = partial.shape[1]
    rows = partial.shape[0] // (2 * GROUP)
    cube = partial.reshape((2, 2, 2, 2, rows, width))

    def fold(values, axis, link):
        low_half = lax.index_in_dim(values, 0, axis, keepdims=False)
        high_half = lax.index_in_dim(values, 1, axis, keepdims=False)
        if link == "x":
            low_half, high_half = ordered(low_half, high_half, tensor_at)
        return low_half.astype(full) + hop(high_half.astype(kind), link).astype(full)

    cube = fold(cube, 0, "core")
    first, second, third = [cube[:, :, :, start:stop] for start, stop in cuts(rows)]
    first = fold(fold(fold(first, 0, "z"), 0, "y"), 0, "x")
    second = fold(fold(fold(second, 2, "x"), 0, "z"), 0, "y")
    third = fold(fold(fold(third, 1, "y"), 1, "x"), 0, "z")
    return jnp.concatenate([first, second, third], axis=0)


def outer_count():
    return lax.axis_size("dp") // GROUP


def outer_groups():
    return [[k + GROUP * other for other in range(outer_count())] for k in range(GROUP)]


def outer_gather(values, axis):
    if outer_count() == 2:
        pieces = ordered(values, hop(values, "outer"), lax.axis_index("dp") // GROUP)
        return jnp.concatenate(pieces, axis=axis)
    return lax.all_gather(values, "dp", axis_index_groups=outer_groups(), axis=axis, tiled=True)


def channel_gather(values):
    if outer_count() == 2:
        return jnp.concatenate([values, hop(values, "outer")], axis=-1)
    return lax.all_gather(
        values, "dp", axis_index_groups=outer_groups(), axis=values.ndim - 1, tiled=True
    )


def channel_scatter(make, width, kind):
    if outer_count() == 2:
        half = width // 2
        got = hop(make(half, width).astype(kind), "outer")
        return make(0, half) + got.astype(full)
    values = make(0, width).astype(kind)
    return lax.psum_scatter(
        values, "dp", axis_index_groups=outer_groups(), scatter_dimension=values.ndim - 1, tiled=True
    ).astype(full)


def outer_sum(make):
    if outer_count() == 2:
        here = lax.axis_index("dp") // GROUP
        got = hop(make(1 - here).astype(low), "outer")
        return make(here) + got.astype(full)
    blocks = jnp.stack([make(k).astype(low) for k in range(outer_count())], axis=0)
    return lax.psum_scatter(
        blocks, "dp", axis_index_groups=outer_groups(), scatter_dimension=0, tiled=True
    )[0].astype(full)


def inner_swap(values):
    groups = [
        [GROUP * outer + k for k in range(GROUP)] for outer in range(outer_count())
    ]
    return lax.all_to_all(
        values, "dp", split_axis=0, concat_axis=0, axis_index_groups=groups, tiled=True
    )


def lanes_of(values, block, count):
    size = values.shape[1] // count
    return lax.dynamic_slice_in_dim(values, block * size, size, axis=1)


def take_in(weight):
    depth, pairs, width = weight.shape
    cut = weight.reshape((depth, pairs, GROUP, width // GROUP)).transpose((2, 0, 1, 3))
    swapped = inner_swap(cut.reshape((GROUP, depth, pairs * width // GROUP)))
    return outer_gather(swapped.reshape((GROUP * depth, -1)), 0)


def give_in(make, depth, pairs, width):
    total = outer_sum(make).astype(low).reshape((GROUP, depth, -1))
    swapped = inner_swap(total).reshape((GROUP, depth, pairs, width // GROUP))
    return swapped.transpose((1, 2, 0, 3)).reshape((depth, pairs, width)).astype(full)


def take_out(weight):
    height, depth = weight.shape
    swapped = inner_swap(weight.reshape((GROUP, height // GROUP, depth)))
    return outer_gather(swapped.transpose((1, 0, 2)).reshape((height // GROUP, GROUP * depth)), 1)


def give_out(make, height, depth):
    total = outer_sum(make).astype(low).reshape((height // GROUP, GROUP, depth))
    return inner_swap(total.transpose((1, 0, 2))).reshape((height, depth)).astype(full)


def feed_forward(stream, gain, gate_up, down):
    hidden_width = down.shape[0]
    scale, normed = normed_rows(stream, gain)
    every = gather_rows(normed)
    pair = matmul(every, gate_up)
    gate = pair[:, :hidden_width]
    up = pair[:, hidden_width:]
    hidden = (jax.nn.silu(gate) * up).astype(low)
    branch = reduce_rows(matmul(hidden, down).astype(low))
    return stream + branch, (scale, every, gate, up, hidden)


def feed_backward(grad, every_grad, stream, kept, gain, gate_up, down):
    scale, every, gate, up, hidden = kept
    count = outer_count()
    hidden_grad = matmul_lanes(every_grad, down)
    pair_grad = jnp.concatenate(
        [hidden_grad * up * silu_slope(gate), hidden_grad * jax.nn.silu(gate)], axis=1
    ).astype(low)
    normed_grad = reduce_rows(matmul_lanes(pair_grad, gate_up).astype(low))
    norm_part, gain_grad = norm_backward(stream, scale, gain, normed_grad)
    depth = gate_up.shape[0] // (count * GROUP)
    in_grad = give_in(
        lambda block: matmul_rows(lanes_of(every, block, count), pair_grad),
        depth, 2, gate_up.shape[1] * GROUP // 2,
    )
    out_grad = give_out(
        lambda block: matmul_rows(hidden, lanes_of(every_grad, block, count)),
        down.shape[0] * GROUP, depth,
    )
    return grad + norm_part, (gain_grad, in_grad, out_grad)


def shifted(values, places):
    if places >= 0:
        pad = jnp.zeros_like(values[:, :places])
        return jnp.concatenate([pad, values[:, : values.shape[1] - places]], axis=1)
    pad = jnp.zeros_like(values[:, :-places])
    return jnp.concatenate([values[:, -places:], pad], axis=1)


def rotated(heads_in, cosine, sine_part):
    half_width = heads_in.shape[-1] // 2
    first_half = heads_in[..., :half_width]
    second_half = heads_in[..., half_width:]
    return jnp.concatenate(
        [
            first_half * cosine - second_half * sine_part,
            second_half * cosine + first_half * sine_part,
        ],
        axis=-1,
    )


def picks(index, count):
    return (index[:, None] == jnp.arange(count, dtype=jnp.int32)[None, :]).astype(low)


def shards(
    tokens, cotangent, lengths, route, place, gain_one, w_in, conv_w, conv_bias, w_x, w_dt, dt_bias, a_log,
    skip, w_out, gain_three, mlp_one_in, mlp_one_out, gain_two, w_qkv, w_o, gain_four, mlp_two_in, mlp_two_out,
):
    dp_count = lax.axis_size("dp")
    dp_at = lax.axis_index("dp")
    tensor_at = lax.axis_index("tensor")
    row_count, model_width = tokens.shape
    own_count = row_count // lax.axis_size("tensor")
    slot = row_count // dp_count
    count = outer_count()
    seqs = lengths.shape[1]
    part = gain_one.shape[0]

    send_sel = picks(route[0], row_count)
    arrive_sel = picks(place[0], row_count)
    own_sel = lax.dynamic_slice_in_dim(arrive_sel, tensor_at * own_count, own_count, axis=0)
    side = jnp.concatenate([gain_one, gain_three, gain_two, gain_four, lengths[0].astype(low)])
    side_width = -(-side.shape[0] // (slot * LANE)) * LANE
    side_rows = jnp.pad(side, (0, slot * side_width - side.shape[0])).reshape((1, slot, side_width))
    outbound = matmul(send_sel, tokens).astype(low).reshape((dp_count, slot, model_width))
    inbound = lax.all_to_all(
        jnp.concatenate([outbound, jnp.broadcast_to(side_rows, (dp_count, slot, side_width))], axis=2),
        "dp", split_axis=0, concat_axis=0, tiled=True,
    )
    stream = matmul(own_sel, inbound[:, :, :model_width].reshape((row_count, model_width)))
    sides = inbound[:, :, model_width:].reshape((dp_count, slot * side_width))
    gains = [
        sides[:, k * part : (k + 1) * part].reshape((model_width,)).astype(full) for k in range(4)
    ]
    gain_mamba, gain_first, gain_attn, gain_second = gains
    all_lengths = sides[:, 4 * part : 4 * part + seqs].astype(full)

    pack_at = dp_at ^ jnp.array([0, 2, 4, 6, 1, 3, 5, 7], jnp.int32)
    pack_sel = (pack_at[:, None] == jnp.arange(dp_count, dtype=jnp.int32)[None, :]).astype(full)
    pack_lengths = jnp.sum(pack_sel[:, :, None] * all_lengths[None], axis=1).astype(jnp.int32)
    seq_ends = jnp.cumsum(pack_lengths, axis=1)
    row_index = jnp.arange(row_count, dtype=jnp.int32)
    segment = jnp.sum((row_index[None, :, None] >= seq_ends[:, None, :]).astype(jnp.int32), axis=2)
    one_hot = segment[:, :, None] == jnp.arange(seqs, dtype=jnp.int32)[None, None, :]
    offset = row_index[None, :] - jnp.sum(
        jnp.where(one_hot, (seq_ends - pack_lengths)[:, None, :], 0), axis=2
    )
    packs = GROUP
    every_count = packs * row_count
    taps = [(offset >= tap).astype(full)[:, :, None] for tap in range(K)]
    keep_mask = taps[1].reshape((every_count, 1))

    small = channel_gather(
        jnp.concatenate(
            [w_x.T, w_dt, conv_w, conv_bias[None], dt_bias[None], a_log, skip[None]], axis=0
        )
    )
    in_pair = channel_gather(w_in)
    channels = in_pair.shape[2]
    in_flat = in_pair.reshape((model_width, 2 * channels))
    select_rows = R + 2 * N
    select_proj = small[:select_rows]
    step_proj = small[select_rows : select_rows + R]
    rest = small[select_rows + R :].astype(full)
    conv_taps = rest[:K]
    conv_shift = rest[K]
    step_bias = rest[K + 1 : K + 2]
    decay_rate = -jnp.exp(rest[K + 2 : K + 2 + N])
    skip_gain = rest[K + 2 + N : K + 3 + N]
    if count == 2:
        out_proj = jnp.concatenate([w_out, hop(w_out, "outer")], axis=0)
    else:
        out_proj = lax.all_gather(w_out, "dp", axis_index_groups=outer_groups(), axis=0, tiled=True)

    scale_mamba, normed_one = normed_rows(stream, gain_mamba)
    every_one = gather_rows(normed_one)
    inner = matmul(every_one, in_flat)
    conv_input = inner[:, :channels].reshape((packs, row_count, channels))
    gate_input = inner[:, channels:]
    conv_sum = conv_shift + conv_taps[0] * conv_input
    for tap in range(1, K):
        conv_sum = conv_sum + conv_taps[tap] * shifted(conv_input, tap) * taps[tap]
    mixer_low = jax.nn.silu(conv_sum).astype(low).reshape((every_count, channels))
    mixer_val = mixer_low.astype(full)
    selected = gather_rows(reduce_rows(matmul_lanes(mixer_low, select_proj)))
    step_low = selected[:, :R].astype(low)
    mats = jnp.pad(selected[:, R:], ((0, 0), (0, LANE - 2 * N)))
    scan_args = (step_low, mats, keep_mask, step_proj, step_bias, decay_rate, skip_gain)
    gated_low, mixer_out, prior = scan_forward(mixer_val, gate_input, *scan_args, packs)
    stream_mid = stream + reduce_rows(matmul(gated_low, out_proj).astype(low))

    first_in = take_in(mlp_one_in)
    first_out = take_out(mlp_one_out)
    stream_ffn, kept_first = feed_forward(stream_mid, gain_first, first_in, first_out)

    proj_flat = take_in(w_qkv)
    attn_out = take_out(w_o)
    inner_width = attn_out.shape[0]
    head_count = inner_width // HD
    scale_attn, normed_two = normed_rows(stream_ffn, gain_attn)
    every_two = gather_rows(normed_two)
    projected = matmul(every_two, proj_flat).reshape((packs, row_count, 3, head_count, HD))
    half_width = HD // 2
    inverse = 10000.0 ** (-jnp.arange(half_width, dtype=full) / half_width)
    angle_table = offset.astype(full)[:, :, None, None] * inverse
    cosine, sine_part = jnp.cos(angle_table), jnp.sin(angle_table)
    factor = float(HD) ** (-0.5)
    query_low = (rotated(projected[:, :, 0], cosine, sine_part) * factor).astype(low)
    key_low = rotated(projected[:, :, 1], cosine, sine_part).astype(low)
    value_low = projected[:, :, 2].astype(low)
    allowed = (segment[:, :, None] == segment[:, None, :]) & (
        row_index[:, None] >= row_index[None, :]
    )
    scores = jnp.einsum("pthd,pshd->phts", query_low, key_low, preferred_element_type=full)
    attn_probs = jax.nn.softmax(jnp.where(allowed[:, None], scores, -1e30), axis=-1)
    probs_low = attn_probs.astype(low)
    context_low = (
        jnp.einsum("phts,pshd->pthd", probs_low, value_low, preferred_element_type=full)
        .astype(low)
        .reshape((every_count, inner_width))
    )
    stream_attn = stream_ffn + reduce_rows(matmul(context_low, attn_out).astype(low))

    second_in = take_in(mlp_two_in)
    second_out = take_out(mlp_two_out)
    result, kept_second = feed_forward(stream_attn, gain_second, second_in, second_out)

    cot_in = lax.all_to_all(
        matmul(send_sel, cotangent).astype(low), "dp", split_axis=0, concat_axis=0, tiled=True
    )
    back_grad = matmul(own_sel, cot_in)
    grad_attn_stream, second_sums = feed_backward(
        back_grad, gather_rows(back_grad.astype(low)), stream_attn, kept_second, gain_second, second_in, second_out
    )

    every_branch = gather_rows(grad_attn_stream.astype(low))
    attn_depth = part
    grad_w_o = give_out(
        lambda block: matmul_rows(context_low, lanes_of(every_branch, block, count)),
        inner_width * GROUP, attn_depth,
    )
    grad_context = (
        matmul_lanes(every_branch, attn_out)
        .astype(low)
        .reshape((packs, row_count, head_count, HD))
    )
    grad_probs = jnp.einsum("pthd,pshd->phts", grad_context, value_low, preferred_element_type=full)
    grad_values = jnp.einsum("phts,pthd->pshd", probs_low, grad_context, preferred_element_type=full)
    grad_scores = (
        attn_probs * (grad_probs - jnp.sum(attn_probs * grad_probs, axis=-1, keepdims=True))
    ).astype(low)
    grad_query = (
        jnp.einsum("phts,pshd->pthd", grad_scores, key_low, preferred_element_type=full) * factor
    )
    grad_key = jnp.einsum("phts,pthd->pshd", grad_scores, query_low, preferred_element_type=full)
    grad_proj = jnp.stack(
        [rotated(grad_query, cosine, -sine_part), rotated(grad_key, cosine, -sine_part), grad_values], axis=2
    )
    grad_proj_low = grad_proj.astype(low).reshape((every_count, 3 * inner_width))
    grad_w_qkv = give_in(
        lambda block: matmul_rows(lanes_of(every_two, block, count), grad_proj_low),
        attn_depth, 3, inner_width * GROUP,
    )
    grad_normed_two = reduce_rows(matmul_lanes(grad_proj_low, proj_flat).astype(low))
    norm_ffn, grad_gain_two = norm_backward(stream_ffn, scale_attn, gain_attn, grad_normed_two)
    grad_ffn_stream = grad_attn_stream + norm_ffn

    grad_mid, first_sums = feed_backward(
        grad_ffn_stream, gather_rows(grad_ffn_stream.astype(low)), stream_mid, kept_first, gain_first,
        first_in, first_out,
    )

    every_mixed = gather_rows(grad_mid.astype(low))
    grad_gated = matmul_lanes(every_mixed, out_proj)
    if count == 2:
        half = channels // 2
        got = hop(matmul_rows(gated_low[:, half:], every_mixed).astype(low), "outer")
        grad_w_out = matmul_rows(gated_low[:, :half], every_mixed) + got.astype(full)
    else:
        grad_w_out = lax.psum_scatter(
            matmul_rows(gated_low, every_mixed).astype(low), "dp", axis_index_groups=outer_groups(),
            scatter_dimension=0, tiled=True,
        ).astype(full)
    grad_step_low, grad_mixer, grad_gate, mats_grad, grad_a_log, grad_skip = scan_backward(
        mixer_val, gate_input, mixer_out, grad_gated, *scan_args, prior, packs
    )
    grad_dt_bias = jnp.sum(grad_step_low.astype(full), axis=0, keepdims=True)
    grad_w_dt = matmul_rows(step_low, grad_step_low)
    grad_selected = gather_rows(
        reduce_rows(
            jnp.concatenate(
                [matmul_lanes(grad_step_low, step_proj), mats_grad[:, 0 : 2 * N : 2], mats_grad[:, 1 : 2 * N : 2]],
                axis=1,
            )
        ).astype(low)
    )
    grad_w_x = matmul_rows(grad_selected, mixer_low)
    grad_mixer = grad_mixer + matmul(grad_selected, select_proj)
    grad_conv = grad_mixer.reshape((packs, row_count, channels)) * silu_slope(conv_sum)
    grad_conv_bias = jnp.sum(grad_conv, axis=(0, 1))[None]
    tap_grads = [jnp.sum(grad_conv * conv_input, axis=(0, 1))]
    grad_conv_input = conv_taps[0] * grad_conv
    for tap in range(1, K):
        masked_grad = grad_conv * taps[tap]
        tap_grads.append(jnp.sum(masked_grad * shifted(conv_input, tap), axis=(0, 1)))
        grad_conv_input = grad_conv_input + conv_taps[tap] * shifted(masked_grad, -tap)
    grad_conv_low = grad_conv_input.astype(low).reshape((every_count, channels))
    grad_inner = jnp.concatenate([grad_conv_low, grad_gate], axis=1)
    grad_normed_one = reduce_rows(matmul_lanes(grad_inner, in_flat).astype(low))

    def in_grads(start, stop):
        columns = jnp.concatenate([grad_conv_low[:, start:stop], grad_gate[:, start:stop]], axis=1)
        return matmul_rows(every_one, columns).reshape((model_width, 2, stop - start))

    grad_w_in = channel_scatter(in_grads, channels, low)
    small_grads = jnp.concatenate(
        [grad_w_x, grad_w_dt, jnp.stack(tap_grads), grad_conv_bias, grad_dt_bias, grad_a_log, grad_skip], axis=0
    )
    small_sums = channel_scatter(lambda start, stop: small_grads[:, start:stop], channels, full)
    norm_in, grad_gain_one = norm_backward(stream, scale_mamba, gain_mamba, grad_normed_one)
    input_grad = grad_mid + norm_in

    def homeward(own_rows):
        pieces = ordered(own_rows, hop(own_rows, "x"), tensor_at)
        packed = jnp.concatenate(pieces, axis=0)
        return matmul_rows(arrive_sel, packed).astype(low).reshape((dp_count, slot, model_width))

    def landed(home):
        return matmul_rows(send_sel, home.reshape((row_count, model_width)))

    final_out = landed(
        lax.all_to_all(homeward(result.astype(low)), "dp", split_axis=0, concat_axis=0, tiled=True)
    )
    gain_grads = jnp.stack([grad_gain_one, first_sums[0], grad_gain_two, second_sums[0]])
    gain_grads = gain_grads + hop(gain_grads, "x")
    gain_high = gain_grads.astype(low)
    gain_parts = jnp.stack([gain_high, (gain_grads - gain_high.astype(full)).astype(low)])
    gain_parts = gain_parts.reshape((8, dp_count, part)).transpose((1, 0, 2)).reshape((dp_count, 8 * part))
    gain_width = -(-8 * part // (slot * LANE)) * LANE
    gain_parts = jnp.pad(gain_parts, ((0, 0), (0, slot * gain_width - 8 * part)))
    gain_parts = gain_parts.reshape((dp_count, slot, gain_width))
    home_grad = lax.all_to_all(
        jnp.concatenate([homeward(input_grad.astype(low)), gain_parts], axis=2),
        "dp", split_axis=0, concat_axis=0, tiled=True,
    )
    final_grad = landed(home_grad[:, :, :model_width])
    gain_sums = jnp.sum(
        home_grad[:, :, model_width:].reshape((dp_count, slot * gain_width))[:, : 8 * part].astype(full), axis=0
    )
    gain_sums = gain_sums.reshape((2, 4, part))
    gain_sums = gain_sums[0] + gain_sums[1]
    sizes = [select_rows, R, K, 1, 1, N, 1]
    cut_at = [sum(sizes[:k]) for k in range(len(sizes) + 1)]
    pieces = [small_sums[cut_at[k] : cut_at[k + 1]] for k in range(len(sizes))]
    return (
        final_out, final_grad, gain_sums[0], grad_w_in, pieces[2], pieces[3][0], pieces[0].T, pieces[1],
        pieces[4][0], pieces[5], pieces[6][0], grad_w_out, gain_sums[1], first_sums[1], first_sums[2],
        gain_sums[2], grad_w_qkv, grad_w_o, gain_sums[3], second_sums[1], second_sums[2],
    )


def solution(mesh):
    return jax.shard_map(
        shards,
        mesh=mesh,
        in_specs=(
            P("dp", None),
            P("dp", None),
            P("dp", None),
            P("dp", None),
            P("dp", None),
            P("dp"),
            P(None, None, ("dp", "tensor")),
            P(None, ("dp", "tensor")),
            P(("dp", "tensor")),
            P(("dp", "tensor"), None),
            P(None, ("dp", "tensor")),
            P(("dp", "tensor")),
            P(None, ("dp", "tensor")),
            P(("dp", "tensor")),
            P(("dp", "tensor"), None),
            P("dp"),
            P("dp", None, "tensor"),
            P("tensor", "dp"),
            P("dp"),
            P("dp", None, "tensor"),
            P("tensor", "dp"),
            P("dp"),
            P("dp", None, "tensor"),
            P("tensor", "dp"),
        ),
        out_specs=(
            P("dp", None),
            P("dp", None),
            P("dp"),
            P(None, None, ("dp", "tensor")),
            P(None, ("dp", "tensor")),
            P(("dp", "tensor")),
            P(("dp", "tensor"), None),
            P(None, ("dp", "tensor")),
            P(("dp", "tensor")),
            P(None, ("dp", "tensor")),
            P(("dp", "tensor")),
            P(("dp", "tensor"), None),
            P("dp"),
            P("dp", None, "tensor"),
            P("tensor", "dp"),
            P("dp"),
            P("dp", None, "tensor"),
            P("tensor", "dp"),
            P("dp"),
            P("dp", None, "tensor"),
            P("tensor", "dp"),
        ),
        check_vma=False,
    )
```

```python
import functools

import jax
import jax.numpy as jnp
from jax import lax
from jax.experimental import pallas as pl
from jax.experimental.pallas import tpu as pltpu
from jax.sharding import PartitionSpec as P

N = 16
R = 128
K = 4
HD = 64
LANE = 128
GROUP = 8
LOG2E = 1.4426950408889634
LN2 = 0.6931471805599453

low = jnp.bfloat16
full = jnp.float32
eps = 1e-05


def block_rows(ref, start, count, stride):
    return ref[pl.ds(start, count, stride=stride), :]


def spread(ref, values):
    rows = values.shape[0]
    for part in range(values.shape[1] // LANE):
        ref[part * rows : (part + 1) * rows, :] = values[:, part * LANE : (part + 1) * LANE]


def gathered(ref, rows):
    return jnp.concatenate(
        [ref[part * rows : (part + 1) * rows, :] for part in range(ref.shape[0] // rows)], axis=1
    )


def scan_forward_kernel(
    packs, chunk, mixer_ref, gate_ref, low_ref, mats_ref, keep_ref, proj_ref, bias_ref, rate_ref, skip_ref,
    gated_ref, out_ref, prior_ref, step_s, drive_s, out_s, rate_s, state,
):
    rows, width = mixer_ref.shape
    span = rows // packs
    parts = width // LANE
    place = pl.program_id(0)

    @pl.when(place == 0)
    def _():
        state[...] = jnp.zeros_like(state)
        pre = jnp.dot(low_ref[...], proj_ref[...], preferred_element_type=jnp.float32) + bias_ref[...]
        step = jax.nn.softplus(pre)
        spread(drive_s, step * mixer_ref[...])
        spread(step_s, jnp.where(keep_ref[...] > 0.0, step, 1e30))
        for n in range(N):
            for part in range(parts):
                rate_s[n, part] = jnp.broadcast_to(
                    rate_ref[n : n + 1, part * LANE : (part + 1) * LANE] * LOG2E, (packs, LANE)
                )

    def one(k, held):
        t = place * chunk + k
        mats = block_rows(mats_ref, t, packs, span)
        step_now = [block_rows(step_s, part * rows + t, packs, span) for part in range(parts)]
        drive_now = [block_rows(drive_s, part * rows + t, packs, span) for part in range(parts)]
        total = [jnp.zeros((packs, LANE), jnp.float32)] * parts
        fresh = []
        for n in range(N):
            source = jnp.broadcast_to(mats[:, n : n + 1], (packs, LANE))
            reader = jnp.broadcast_to(mats[:, N + n : N + n + 1], (packs, LANE))
            for part in range(parts):
                before = held[n * parts + part]
                prior_ref[k, n, part] = before
                now = jnp.exp2(step_now[part] * rate_s[n, part]) * before + drive_now[part] * source
                total[part] = total[part] + reader * now
                fresh.append(now)
        for part in range(parts):
            out_s[pl.ds(part * rows + t, packs, stride=span), :] = total[part]
        return tuple(fresh)

    final = lax.fori_loop(
        0, chunk, one, tuple(state[n, part] for n in range(N) for part in range(parts))
    )
    for n in range(N):
        for part in range(parts):
            state[n, part] = final[n * parts + part]

    @pl.when(place == pl.num_programs(0) - 1)
    def _():
        mixed = gathered(out_s, rows) + skip_ref[...] * mixer_ref[...]
        out_ref[...] = mixed
        gate = gate_ref[...]
        gated_ref[...] = (mixed * gate * jax.nn.sigmoid(gate)).astype(jnp.bfloat16)


def whole_block(shape):
    return pl.BlockSpec(shape, lambda c: (0,) * len(shape))


def scan_forward(mixer, gate, low, mats, keep, proj, bias, rate, skip, packs, chunk=16):
    rows, width = mixer.shape
    span = rows // packs
    parts = width // LANE
    args = (mixer, gate, low, mats, keep, proj, bias, rate, skip)
    return pl.pallas_call(
        functools.partial(scan_forward_kernel, packs, chunk),
        grid=(span // chunk,),
        in_specs=[whole_block(value.shape) for value in args],
        out_specs=[
            whole_block((rows, width)),
            whole_block((rows, width)),
            pl.BlockSpec((chunk, N, parts, packs, LANE), lambda c: (c, 0, 0, 0, 0)),
        ],
        out_shape=[
            jax.ShapeDtypeStruct((rows, width), jnp.bfloat16),
            jax.ShapeDtypeStruct((rows, width), jnp.float32),
            jax.ShapeDtypeStruct((span, N, parts, packs, LANE), jnp.float32),
        ],
        scratch_shapes=[
            pltpu.VMEM((parts * rows, LANE), jnp.float32),
            pltpu.VMEM((parts * rows, LANE), jnp.float32),
            pltpu.VMEM((parts * rows, LANE), jnp.float32),
            pltpu.VMEM((N, parts, packs, LANE), jnp.float32),
            pltpu.VMEM((N, parts, packs, LANE), jnp.float32),
        ],
        compiler_params=pltpu.CompilerParams(vmem_limit_bytes=48 << 20),
        cost_estimate=pl.CostEstimate(
            flops=rows * width * N * 8, bytes_accessed=rows * width * N * 4, transcendentals=rows * width * N
        ),
    )(*args)


def scan_backward_kernel(
    packs, chunk, mixer_ref, gate_ref, mixed_ref, gated_ref, low_ref, mats_ref, keep_ref, proj_ref, bias_ref,
    rate_ref, skip_ref, prior_ref,
    step_grad_ref, mixer_grad_ref, gate_grad_ref, mats_grad_ref, log_grad_ref, skip_grad_ref,
    step_s, drive_s, mix_s, grad_s, rate_s, total_s, along_s, log_s, state,
):
    rows, width = mixer_ref.shape
    span = rows // packs
    parts = width // LANE
    place = pl.program_id(0)
    lane = lax.broadcasted_iota(jnp.int32, (packs, LANE), 1)

    def step_before():
        return (
            jnp.dot(low_ref[...], proj_ref[...], preferred_element_type=jnp.float32) + bias_ref[...]
        )

    @pl.when(place == 0)
    def _():
        state[...] = jnp.zeros_like(state)
        log_s[...] = jnp.zeros_like(log_s)
        step = jax.nn.softplus(step_before())
        mixer = mixer_ref[...]
        gate = gate_ref[...]
        sig = jax.nn.sigmoid(gate)
        grad = gated_ref[...]
        scan_grad = grad * gate * sig
        gate_grad_ref[...] = (grad * mixed_ref[...] * sig * (1.0 + gate * (1.0 - sig))).astype(jnp.bfloat16)
        skip_grad_ref[...] = jnp.sum(scan_grad * mixer, axis=0, keepdims=True)
        spread(grad_s, scan_grad)
        spread(mix_s, mixer)
        spread(drive_s, step * mixer)
        spread(step_s, jnp.where(keep_ref[...] > 0.0, step, 1e30))
        for n in range(N):
            for part in range(parts):
                rate_s[n, part] = jnp.broadcast_to(
                    rate_ref[n : n + 1, part * LANE : (part + 1) * LANE] * LOG2E, (packs, LANE)
                )

    def one(back, held):
        k = chunk - 1 - back
        t = (pl.num_programs(0) - 1 - place) * chunk + k
        mats = block_rows(mats_ref, t, packs, span)
        step_now = [block_rows(step_s, part * rows + t, packs, span) for part in range(parts)]
        drive_now = [block_rows(drive_s, part * rows + t, packs, span) for part in range(parts)]
        mix_now = [block_rows(mix_s, part * rows + t, packs, span) for part in range(parts)]
        grad_now = [block_rows(grad_s, part * rows + t, packs, span) for part in range(parts)]
        zero = jnp.zeros((packs, LANE), jnp.float32)
        along = [zero] * parts
        rated = [zero] * parts
        source_sums = []
        reader_sums = []
        fresh = []
        for n in range(N):
            source = jnp.broadcast_to(mats[:, n : n + 1], (packs, LANE))
            reader = jnp.broadcast_to(mats[:, N + n : N + n + 1], (packs, LANE))
            source_sum = zero
            reader_sum = zero
            for part in range(parts):
                rate = rate_s[n, part]
                decay = jnp.exp2(step_now[part] * rate)
                kept = decay * prior_ref[k, n, part]
                now = kept + drive_now[part] * source
                adjoint = grad_now[part] * reader + held[n * parts + part]
                fresh.append(decay * adjoint)
                through = adjoint * kept
                rated[part] = rated[part] + through * rate
                log_s[n, part] += through * step_now[part]
                along[part] = along[part] + adjoint * source
                source_sum = source_sum + adjoint * drive_now[part]
                reader_sum = reader_sum + grad_now[part] * now
            source_sums.append(source_sum)
            reader_sums.append(reader_sum)
        for part in range(parts):
            total_s[pl.ds(part * rows + t, packs, stride=span), :] = rated[part] * LN2 + mix_now[part] * along[part]
            along_s[pl.ds(part * rows + t, packs, stride=span), :] = along[part]
        big = jnp.dot(jnp.concatenate(source_sums + reader_sums, axis=0).astype(jnp.bfloat16), jnp.ones((LANE, LANE), jnp.bfloat16), preferred_element_type=jnp.float32)
        mats_grad = zero
        for q in range(2 * N):
            mats_grad = jnp.where(lane == q, big[q * packs : (q + 1) * packs], mats_grad)
        mats_grad_ref[pl.ds(t, packs, stride=span), :] = mats_grad
        return tuple(fresh)

    final = lax.fori_loop(
        0, chunk, one, tuple(state[n, part] for n in range(N) for part in range(parts))
    )
    for n in range(N):
        for part in range(parts):
            state[n, part] = final[n * parts + part]

    @pl.when(place == pl.num_programs(0) - 1)
    def _():
        pre = step_before()
        step_grad_ref[...] = (gathered(total_s, rows) * jax.nn.sigmoid(pre)).astype(jnp.bfloat16)
        mixer_grad_ref[...] = (
            gathered(along_s, rows) * jax.nn.softplus(pre) + skip_ref[...] * gathered(grad_s, rows)
        )
        for n in range(N):
            log_grad_ref[n : n + 1, :] = jnp.concatenate(
                [jnp.sum(log_s[n, part], axis=0, keepdims=True) for part in range(parts)], axis=1
            ) * rate_ref[n : n + 1, :]


def scan_backward(
    mixer, gate, mixed, gated_grad, low, mats, keep, proj, bias, rate, skip, prior, packs, chunk=16
):
    rows, width = mixer.shape
    span = rows // packs
    parts = width // LANE
    last = span // chunk - 1
    args = (mixer, gate, mixed, gated_grad, low, mats, keep, proj, bias, rate, skip)
    shapes = [
        ((rows, width), jnp.bfloat16),
        ((rows, width), jnp.float32),
        ((rows, width), jnp.bfloat16),
        ((rows, LANE), jnp.float32),
        ((N, width), jnp.float32),
        ((1, width), jnp.float32),
    ]
    long_row = pltpu.VMEM((parts * rows, LANE), jnp.float32)
    small = pltpu.VMEM((N, parts, packs, LANE), jnp.float32)
    return pl.pallas_call(
        functools.partial(scan_backward_kernel, packs, chunk),
        grid=(span // chunk,),
        in_specs=[whole_block(value.shape) for value in args]
        + [pl.BlockSpec((chunk, N, parts, packs, LANE), lambda c: (last - c, 0, 0, 0, 0))],
        out_specs=[whole_block(shape) for shape, kind in shapes],
        out_shape=[jax.ShapeDtypeStruct(shape, kind) for shape, kind in shapes],
        scratch_shapes=[long_row, long_row, long_row, long_row, small, long_row, long_row, small, small],
        compiler_params=pltpu.CompilerParams(vmem_limit_bytes=56 << 20),
        cost_estimate=pl.CostEstimate(
            flops=rows * width * N * 20, bytes_accessed=rows * width * N * 4, transcendentals=rows * width * N
        ),
    )(*args, prior)


def silu_slope(operand):
    sig_value = jax.nn.sigmoid(operand)
    return sig_value * (1.0 + operand * (1.0 - sig_value))


def matmul(left, right):
    return jnp.dot(left, right, preferred_element_type=full)


def matmul_rows(left, right):
    return lax.dot_general(left, right, (((0,), (0,)), ((), ())), preferred_element_type=full)


def matmul_lanes(left, right):
    return lax.dot_general(left, right, (((1,), (1,)), ((), ())), preferred_element_type=full)


def norm_scale(stream):
    return lax.rsqrt(jnp.mean(stream * stream, axis=-1, keepdims=True) + eps)


def normed_rows(stream, gain):
    scale = norm_scale(stream)
    return scale, (stream * scale * gain[None, :]).astype(low)


def norm_backward(stream, rms_scale, gain_vec, grad_normed):
    weighted = grad_normed * gain_vec[None, :]
    inner_mean = jnp.mean(weighted * stream, axis=-1, keepdims=True)
    grad_stream = rms_scale * weighted - stream * rms_scale * rms_scale * rms_scale * inner_mean
    return (grad_stream, jnp.sum(grad_normed * stream * rms_scale, axis=0))


def hop(values, link):
    if link == "x":
        return lax.ppermute(values, "tensor", [(0, 1), (1, 0)])
    dp_count = lax.axis_size("dp")
    bit = {"core": 1, "y": 2, "outer": 4, "z": dp_count // 2}[link]
    return lax.ppermute(values, "dp", [(k, k ^ bit) for k in range(dp_count)])


def ordered(mine, theirs, index):
    first = index == 0
    return jnp.where(first, mine, theirs), jnp.where(first, theirs, mine)


def gather_rows(own):
    tensor_at = lax.axis_index("tensor")
    by_z = hop(own, "z")
    by_x = hop(own, "x")
    by_y = hop(own, "y")
    by_xz = hop(by_z, "x")
    by_yz = hop(by_z, "y")
    by_xy = hop(by_y, "x")
    by_xyz = hop(by_xz, "y")
    pairs = [(own, by_x), (by_y, by_xy), (by_z, by_xz), (by_yz, by_xyz)]
    local = jnp.concatenate(
        [piece for near, far in pairs for piece in ordered(near, far, tensor_at)], axis=0
    )
    return jnp.concatenate([local, hop(local, "core")], axis=0)


def reduce_rows(partial):
    kind = partial.dtype
    tensor_at = lax.axis_index("tensor")
    half = partial.shape[0] // 2
    rows = half // GROUP
    mine = partial[:half]
    mate = hop(partial[half:], "core")

    def block(z, y, x):
        pieces = []
        for side in range(2):
            at = (4 * z + 2 * y + side) * rows
            pieces.append(mine[at : at + rows].astype(full) + mate[at : at + rows].astype(full))
        return ordered(pieces[0], pieces[1], tensor_at)[x]

    def send(values, link):
        return hop(values.astype(kind), link).astype(full)

    from_xyz = send(block(1, 1, 1), "y")
    from_xy = send(block(0, 1, 1), "x")
    from_yz = send(block(1, 1, 0), "y")
    from_xz = send(block(1, 0, 1) + from_xyz, "x")
    from_x = send(block(0, 0, 1), "x")
    from_y = send(block(0, 1, 0) + from_xy, "y")
    from_z = send(block(1, 0, 0) + from_yz + from_xz, "z")
    return block(0, 0, 0) + from_x + from_y + from_z


def total_rows(partial):
    half = partial.shape[0] // 2
    rows = half // GROUP
    mine = partial[:half] + hop(partial[half:], "core")
    cube = mine.reshape((2, 2, 2, rows, partial.shape[1]))
    third = rows * 3 // 8
    parts = []
    for start, stop, order in ((0, third, "xyz"), (third, 2 * third, "yzx"), (2 * third, rows, "zxy")):
        part = cube[:, :, :, start:stop]
        for link in order:
            sent = part if link == "x" else jnp.flip(part, 0 if link == "z" else 1)
            part = part + hop(sent, link)
        parts.append(part)
    mine = jnp.concatenate(parts, axis=3).reshape((half, partial.shape[1]))
    return jnp.concatenate([mine, hop(mine, "core")], axis=0)


def outer_count():
    return lax.axis_size("dp") // GROUP


def outer_at():
    return lax.axis_index("dp") % (lax.axis_size("dp") // 2) // 4


def inner_groups():
    half = lax.axis_size("dp") // 2
    return [
        [half * side + 4 * outer + k for side in range(2) for k in range(4)] for outer in range(outer_count())
    ]


def outer_groups():
    return [list(members) for members in zip(*inner_groups())]


def regrouped(values, axis, back=False):
    shape = values.shape
    split = (outer_count(), 2) if back else (2, outer_count())
    values = values.reshape(shape[:axis] + split + (-1,) + shape[axis + 1 :])
    return jnp.swapaxes(values, axis, axis + 1).reshape(shape)


def outer_gather(values, axis):
    return lax.all_gather(values, "dp", axis_index_groups=outer_groups(), axis=axis, tiled=True)


def outer_scatter(values, axis):
    return lax.psum_scatter(
        values, "dp", axis_index_groups=outer_groups(), scatter_dimension=axis, tiled=True
    )


def inner_swap(values):
    return lax.all_to_all(
        values, "dp", split_axis=0, concat_axis=0, axis_index_groups=inner_groups(), tiled=True
    )


def pack_kernel(in_ref, out_ref, packed_ref):
    pairs, width = in_ref.shape[1:]
    for k in range(pairs):
        packed_ref[0, :, k * width : (k + 1) * width] = in_ref[:, k, :]
    packed_ref[0, :, pairs * width :] = out_ref[...].T


def pack_weights(inward, outward):
    depth, pairs, width = inward.shape
    width = width // GROUP
    height = outward.shape[0] // GROUP
    total = pairs * width + height
    return pl.pallas_call(
        pack_kernel,
        grid=(GROUP,),
        in_specs=[
            pl.BlockSpec((depth, pairs, width), lambda k: (0, 0, k)),
            pl.BlockSpec((height, depth), lambda k: (k, 0)),
        ],
        out_specs=pl.BlockSpec((1, depth, total), lambda k: (k, 0, 0)),
        out_shape=jax.ShapeDtypeStruct((GROUP, depth, total), low),
        compiler_params=pltpu.CompilerParams(vmem_limit_bytes=40 << 20),
        cost_estimate=pl.CostEstimate(
            flops=0, bytes_accessed=4 * GROUP * depth * total, transcendentals=0
        ),
    )(inward, outward)


def unpack_kernel(packed_ref, in_ref, out_ref):
    values = packed_ref[0].astype(full)
    pairs, width = in_ref.shape[1:]
    for k in range(pairs):
        in_ref[:, k, :] = values[:, k * width : (k + 1) * width]
    out_ref[...] = values[:, pairs * width :].T


def unpack_grads(packed, pairs, height):
    depth, total = packed.shape[1:]
    width = (total - height) // pairs
    return pl.pallas_call(
        unpack_kernel,
        grid=(GROUP,),
        in_specs=[pl.BlockSpec((1, depth, total), lambda k: (k, 0, 0))],
        out_specs=[
            pl.BlockSpec((depth, pairs, width), lambda k: (0, 0, k)),
            pl.BlockSpec((height, depth), lambda k: (k, 0)),
        ],
        out_shape=[
            jax.ShapeDtypeStruct((depth, pairs, GROUP * width), full),
            jax.ShapeDtypeStruct((GROUP * height, depth), full),
        ],
        compiler_params=pltpu.CompilerParams(vmem_limit_bytes=40 << 20),
        cost_estimate=pl.CostEstimate(
            flops=0, bytes_accessed=6 * GROUP * depth * total, transcendentals=0
        ),
    )(packed)


def widen_kernel(in_ref, out_ref):
    values = in_ref[...].astype(full)
    pairs, width = out_ref.shape[1:]
    for k in range(pairs):
        out_ref[:, k, :] = values[:, k * width : (k + 1) * width]


def widen(values, pairs):
    depth, wide = values.shape
    width = wide // pairs
    rows = depth // 8
    return pl.pallas_call(
        widen_kernel,
        grid=(8,),
        in_specs=[pl.BlockSpec((rows, wide), lambda k: (k, 0))],
        out_specs=pl.BlockSpec((rows, pairs, width), lambda k: (k, 0, 0)),
        out_shape=jax.ShapeDtypeStruct((depth, pairs, width), full),
        compiler_params=pltpu.CompilerParams(vmem_limit_bytes=40 << 20),
        cost_estimate=pl.CostEstimate(flops=0, bytes_accessed=6 * depth * wide, transcendentals=0),
    )(values)


def tie(values, event):
    zero = jnp.minimum(jnp.abs(event[(slice(0, 1),) * event.ndim].astype(full)), 0.0).reshape(())
    return values + zero.astype(values.dtype)


def queued_gather(swapped, pieces, event):
    values = swapped.reshape((-1, swapped.shape[2]))
    width = values.shape[1] // pieces
    got = []
    for k in range(pieces):
        event = outer_gather(tie(values[:, k * width : (k + 1) * width], event), 0)
        got.append(event)
    return got


def outer_total(total):
    mine = outer_scatter(total.astype(low), 0)
    return mine.reshape((GROUP, -1, mine.shape[1]))


def feed_forward(stream, normed, scale, weights):
    hidden_width = weights.shape[1] // 3
    every = gather_rows(normed)
    pair = matmul(every, weights[:, : 2 * hidden_width])
    gate = pair[:, :hidden_width]
    up = pair[:, hidden_width:]
    hidden = (jax.nn.silu(gate) * up).astype(low)
    branch = reduce_rows(matmul_lanes(hidden, weights[:, 2 * hidden_width :]).astype(low))
    return stream + branch, (scale, every, gate, up, hidden)


def feed_backward(grad, every_grad, stream, kept, gain, weights):
    scale, every, gate, up, hidden = kept
    hidden_width = hidden.shape[1]
    hidden_grad = matmul(every_grad, weights[:, 2 * hidden_width :])
    pair_grad = jnp.concatenate(
        [hidden_grad * up * silu_slope(gate), hidden_grad * jax.nn.silu(gate)], axis=1
    ).astype(low)
    normed_grad = reduce_rows(matmul_lanes(pair_grad, weights[:, : 2 * hidden_width]).astype(low))
    norm_part, gain_grad = norm_backward(stream, scale, gain, normed_grad)
    out_grad = outer_total(matmul_rows(every_grad, hidden))
    in_grad = outer_total(matmul_rows(every, pair_grad))
    return grad + norm_part, gain_grad, jnp.concatenate([in_grad, out_grad], axis=2)


def shifted(values, places):
    if places >= 0:
        pad = jnp.zeros_like(values[:, :places])
        return jnp.concatenate([pad, values[:, : values.shape[1] - places]], axis=1)
    pad = jnp.zeros_like(values[:, :-places])
    return jnp.concatenate([values[:, -places:], pad], axis=1)


def rotated(heads_in, cosine, sine_part):
    half_width = heads_in.shape[-1] // 2
    first_half = heads_in[..., :half_width]
    second_half = heads_in[..., half_width:]
    return jnp.concatenate(
        [
            first_half * cosine - second_half * sine_part,
            second_half * cosine + first_half * sine_part,
        ],
        axis=-1,
    )


def picks(index, count):
    return (index[:, None] == jnp.arange(count, dtype=jnp.int32)[None, :]).astype(low)


def shards(
    tokens, cotangent, lengths, route, place, gain_one, w_in, conv_w, conv_bias, w_x, w_dt, dt_bias, a_log,
    skip, w_out, gain_three, mlp_one_in, mlp_one_out, gain_two, w_qkv, w_o, gain_four, mlp_two_in, mlp_two_out,
):
    dp_count = lax.axis_size("dp")
    dp_at = lax.axis_index("dp")
    tensor_at = lax.axis_index("tensor")
    row_count, model_width = tokens.shape
    own_count = row_count // lax.axis_size("tensor")
    slot = row_count // dp_count
    count = outer_count()
    seqs = lengths.shape[1]
    part = gain_one.shape[0]

    send_sel = picks(route[0], row_count)
    arrive_sel = picks(place[0], row_count)
    own_sel = lax.dynamic_slice_in_dim(arrive_sel, tensor_at * own_count, own_count, axis=0)
    side = jnp.concatenate([gain_one, gain_three, gain_two, gain_four, lengths[0].astype(low)])
    side_width = -(-side.shape[0] // (slot * LANE)) * LANE
    side_rows = jnp.pad(side, (0, slot * side_width - side.shape[0])).reshape((1, slot, side_width))
    outbound = matmul(send_sel, tokens).astype(low).reshape((dp_count, slot, model_width))
    inbound = lax.all_to_all(
        jnp.concatenate([outbound, jnp.broadcast_to(side_rows, (dp_count, slot, side_width))], axis=2),
        "dp", split_axis=0, concat_axis=0, tiled=True,
    )
    stream = matmul(own_sel, inbound[:, :, :model_width].reshape((row_count, model_width)))
    stream = regrouped(stream, 1)
    sides = inbound[:, :, model_width:].reshape((dp_count, slot * side_width))
    gains = [
        regrouped(sides[:, k * part : (k + 1) * part].reshape((model_width,)), 0).astype(full)
        for k in range(4)
    ]
    gain_mamba, gain_first, gain_attn, gain_second = gains
    all_lengths = sides[:, 4 * part : 4 * part + seqs].astype(full)

    side_bit = dp_count // 2
    pack_at = dp_at ^ jnp.array(
        [core + 2 * y + side_bit * z for core in range(2) for z in range(2) for y in range(2)], jnp.int32
    )
    pack_sel = (pack_at[:, None] == jnp.arange(dp_count, dtype=jnp.int32)[None, :]).astype(full)
    pack_lengths = jnp.sum(pack_sel[:, :, None] * all_lengths[None], axis=1).astype(jnp.int32)
    seq_ends = jnp.cumsum(pack_lengths, axis=1)
    row_index = jnp.arange(row_count, dtype=jnp.int32)
    segment = jnp.sum((row_index[None, :, None] >= seq_ends[:, None, :]).astype(jnp.int32), axis=2)
    one_hot = segment[:, :, None] == jnp.arange(seqs, dtype=jnp.int32)[None, None, :]
    offset = row_index[None, :] - jnp.sum(
        jnp.where(one_hot, (seq_ends - pack_lengths)[:, None, :], 0), axis=2
    )
    packs = GROUP
    every_count = packs * row_count
    taps = [(offset >= tap).astype(full)[:, :, None] for tap in range(K)]
    keep_mask = taps[1].reshape((every_count, 1))

    block = w_in.shape[2]
    channels = count * block
    in_blocks = outer_gather(w_in[None], 0)
    in_flat = regrouped(in_blocks.transpose((1, 0, 2, 3)), 0).reshape((model_width, 2 * channels))
    small = jnp.concatenate(
        [w_x.T, w_dt, conv_w, conv_bias[None], dt_bias[None], a_log, skip[None]], axis=0
    )
    if count == 2:
        small = jnp.concatenate(ordered(small, hop(small, "outer"), outer_at()), axis=1)
    else:
        small = outer_gather(small, 1)
    select_rows = R + 2 * N
    select_proj = small[:select_rows]
    step_proj = small[select_rows : select_rows + R]
    rest = small[select_rows + R :].astype(full)
    conv_taps = rest[:K]
    conv_shift = rest[K]
    step_bias = rest[K + 1 : K + 2]
    decay_rate = -jnp.exp(rest[K + 2 : K + 2 + N])
    skip_gain = rest[K + 2 + N : K + 3 + N]

    first_swapped = inner_swap(pack_weights(mlp_one_in, mlp_one_out))
    first_pieces = queued_gather(first_swapped, 3, in_blocks)
    first_weights = jnp.concatenate(first_pieces, axis=1)
    out_proj = regrouped(outer_gather(tie(w_out, first_pieces[1]), 0), 1)
    scale_mamba, normed_one = normed_rows(stream, gain_mamba)
    every_one = gather_rows(normed_one)
    inner = matmul(every_one, in_flat).reshape((every_count, count, 2, block))
    conv_input = inner[:, :, 0].reshape((packs, row_count, channels))
    gate_input = inner[:, :, 1].reshape((every_count, channels))
    conv_sum = conv_shift + conv_taps[0] * conv_input
    for tap in range(1, K):
        conv_sum = conv_sum + conv_taps[tap] * shifted(conv_input, tap) * taps[tap]
    mixer_low = jax.nn.silu(conv_sum).astype(low).reshape((every_count, channels))
    mixer_val = mixer_low.astype(full)
    selected = total_rows(tie(matmul_lanes(mixer_low, select_proj), first_swapped))
    attn_swapped = inner_swap(tie(pack_weights(w_qkv, w_o), selected))
    attn_pieces = queued_gather(attn_swapped, 1, first_pieces[-1])
    attn_weights = jnp.concatenate(attn_pieces, axis=1)
    step_low = selected[:, :R].astype(low)
    mats = jnp.pad(selected[:, R:], ((0, 0), (0, LANE - 2 * N)))
    scan_args = (step_low, mats, keep_mask, step_proj, step_bias, decay_rate, skip_gain)
    gated_low, mixer_out, prior = scan_forward(mixer_val, gate_input, *scan_args, packs)
    stream_mid = stream + reduce_rows(tie(matmul(gated_low, out_proj).astype(low), attn_swapped))

    second_swapped = inner_swap(tie(pack_weights(mlp_two_in, mlp_two_out), stream_mid))
    second_pieces = queued_gather(second_swapped, 3, attn_pieces[-1])
    second_weights = jnp.concatenate(second_pieces, axis=1)
    scale_first, normed_first = normed_rows(stream_mid, gain_first)
    stream_ffn, kept_first = feed_forward(stream_mid, normed_first, scale_first, first_weights)

    inner_width = w_o.shape[0] // GROUP
    proj_flat = attn_weights[:, : 3 * inner_width]
    attn_out = attn_weights[:, 3 * inner_width :]
    head_count = inner_width // HD
    scale_attn, normed_two = normed_rows(stream_ffn, gain_attn)
    every_two = gather_rows(normed_two)
    projected = matmul(every_two, proj_flat).reshape((packs, row_count, 3, head_count, HD))
    half_width = HD // 2
    inverse = 10000.0 ** (-jnp.arange(half_width, dtype=full) / half_width)
    angle_table = offset.astype(full)[:, :, None, None] * inverse
    cosine, sine_part = jnp.cos(angle_table), jnp.sin(angle_table)
    factor = float(HD) ** (-0.5)
    query_low = (rotated(projected[:, :, 0], cosine, sine_part) * factor).astype(low)
    key_low = rotated(projected[:, :, 1], cosine, sine_part).astype(low)
    value_low = projected[:, :, 2].astype(low)
    allowed = (segment[:, :, None] == segment[:, None, :]) & (
        row_index[:, None] >= row_index[None, :]
    )
    scores = jnp.einsum("pthd,pshd->phts", query_low, key_low, preferred_element_type=full)
    attn_probs = jax.nn.softmax(jnp.where(allowed[:, None], scores, -1e30), axis=-1)
    probs_low = attn_probs.astype(low)
    context_low = (
        jnp.einsum("phts,pshd->pthd", probs_low, value_low, preferred_element_type=full)
        .astype(low)
        .reshape((every_count, inner_width))
    )
    stream_attn = stream_ffn + reduce_rows(matmul_lanes(context_low, attn_out).astype(low))

    scale_second, normed_second = normed_rows(stream_attn, gain_second)
    result, kept_second = feed_forward(stream_attn, normed_second, scale_second, second_weights)

    cot_in = lax.all_to_all(
        matmul(send_sel, cotangent).astype(low), "dp", split_axis=0, concat_axis=0, tiled=True
    )
    back_grad = regrouped(matmul(own_sel, cot_in), 1)
    every_back = gather_rows(back_grad.astype(low))
    grad_attn_stream, grad_gain_second, second_total = feed_backward(
        back_grad, every_back, stream_attn, kept_second, gain_second, second_weights
    )

    every_branch = gather_rows(grad_attn_stream.astype(low))
    grad_context = (
        matmul(every_branch, attn_out)
        .astype(low)
        .reshape((packs, row_count, head_count, HD))
    )
    grad_probs = jnp.einsum("pthd,pshd->phts", grad_context, value_low, preferred_element_type=full)
    grad_values = jnp.einsum("phts,pthd->pshd", probs_low, grad_context, preferred_element_type=full)
    grad_scores = (
        attn_probs * (grad_probs - jnp.sum(attn_probs * grad_probs, axis=-1, keepdims=True))
    ).astype(low)
    grad_query = (
        jnp.einsum("phts,pshd->pthd", grad_scores, key_low, preferred_element_type=full) * factor
    )
    grad_key = jnp.einsum("phts,pthd->pshd", grad_scores, query_low, preferred_element_type=full)
    grad_proj = jnp.stack(
        [rotated(grad_query, cosine, -sine_part), rotated(grad_key, cosine, -sine_part), grad_values], axis=2
    )
    grad_proj_low = grad_proj.astype(low).reshape((every_count, 3 * inner_width))
    attn_total = outer_total(
        jnp.concatenate([matmul_rows(every_two, grad_proj_low), matmul_rows(every_branch, context_low)], axis=1)
    )
    grad_normed_two = reduce_rows(matmul_lanes(grad_proj_low, proj_flat).astype(low))
    norm_ffn, grad_gain_two = norm_backward(stream_ffn, scale_attn, gain_attn, grad_normed_two)
    grad_ffn_stream = grad_attn_stream + norm_ffn

    grad_mid, grad_gain_first, first_total = feed_backward(
        grad_ffn_stream, gather_rows(grad_ffn_stream.astype(low)), stream_mid, kept_first, gain_first, first_weights
    )

    every_mixed = gather_rows(grad_mid.astype(low))
    grad_gated = matmul_lanes(every_mixed, out_proj)
    grad_w_out = outer_scatter(matmul_rows(gated_low, every_mixed).astype(low), 0)
    grad_w_out = regrouped(grad_w_out, 1, True).astype(full)
    grad_step_low, grad_mixer, grad_gate, mats_grad, grad_a_log, grad_skip = scan_backward(
        mixer_val, gate_input, mixer_out, grad_gated, *scan_args, prior, packs
    )
    second_grads = inner_swap(tie(second_total, grad_gated))
    grad_dt_bias = jnp.sum(grad_step_low.astype(full), axis=0, keepdims=True)
    grad_w_dt = matmul_rows(step_low, grad_step_low)
    grad_selected = total_rows(
        tie(
            jnp.concatenate([matmul_lanes(grad_step_low, step_proj), mats_grad[:, : 2 * N]], axis=1),
            second_grads,
        )
    ).astype(low)
    attn_grads = inner_swap(tie(attn_total, grad_selected))
    grad_w_x = matmul_rows(grad_selected, mixer_low)
    grad_mixer = grad_mixer + matmul(grad_selected, select_proj)
    grad_conv = grad_mixer.reshape((packs, row_count, channels)) * silu_slope(conv_sum)
    grad_conv_bias = jnp.sum(grad_conv, axis=(0, 1))[None]
    tap_grads = [jnp.sum(grad_conv * conv_input, axis=(0, 1))]
    grad_conv_input = conv_taps[0] * grad_conv
    for tap in range(1, K):
        masked_grad = grad_conv * taps[tap]
        tap_grads.append(jnp.sum(masked_grad * shifted(conv_input, tap), axis=(0, 1)))
        grad_conv_input = grad_conv_input + conv_taps[tap] * shifted(masked_grad, -tap)
    grad_conv_low = grad_conv_input.astype(low).reshape((every_count, channels))
    grad_inner = jnp.stack(
        [grad_conv_low.reshape((every_count, count, block)), grad_gate.reshape((every_count, count, block))], axis=2
    ).reshape((every_count, 2 * channels))
    grad_normed_one = reduce_rows(
        tie(matmul_lanes(grad_inner, in_flat).astype(low), attn_grads)
    )

    in_total = jnp.concatenate(
        [
            matmul_rows(every_one, grad_inner[:, 2 * block * k : 2 * block * (k + 1)]).astype(low)
            for k in range(count)
        ],
        axis=0,
    )
    grad_w_in = widen(regrouped(outer_scatter(in_total, 0), 0, True), 2)
    small_grads = jnp.concatenate(
        [grad_w_x, grad_w_dt, jnp.stack(tap_grads), grad_conv_bias, grad_dt_bias, grad_a_log, grad_skip], axis=0
    )
    if count == 2:
        here = outer_at()
        theirs = lax.dynamic_slice_in_dim(small_grads, (1 - here) * block, block, axis=1)
        small_sums = lax.dynamic_slice_in_dim(small_grads, here * block, block, axis=1) + hop(theirs, "outer")
    else:
        small_sums = outer_scatter(small_grads, 1)
    first_grads = inner_swap(first_total)
    grad_one_in, grad_one_out = unpack_grads(first_grads, 2, mlp_one_out.shape[0] // GROUP)
    grad_two_in, grad_two_out = unpack_grads(second_grads, 2, mlp_two_out.shape[0] // GROUP)
    grad_w_qkv, grad_w_o = unpack_grads(attn_grads, 3, inner_width)
    norm_in, grad_gain_one = norm_backward(stream, scale_mamba, gain_mamba, grad_normed_one)
    input_grad = grad_mid + norm_in

    def homeward(own_rows):
        pieces = ordered(own_rows, hop(own_rows, "x"), tensor_at)
        packed = jnp.concatenate(pieces, axis=0)
        return matmul_rows(arrive_sel, packed).astype(low).reshape((dp_count, slot, model_width))

    def landed(home):
        return regrouped(matmul_rows(send_sel, home.reshape((row_count, model_width))), 1, True)

    final_out = landed(
        lax.all_to_all(homeward(result.astype(low)), "dp", split_axis=0, concat_axis=0, tiled=True)
    )
    gain_grads = jnp.stack([grad_gain_one, grad_gain_first, grad_gain_two, grad_gain_second])
    gain_grads = regrouped(gain_grads + hop(gain_grads, "x"), 1, True)
    gain_high = gain_grads.astype(low)
    gain_parts = jnp.stack([gain_high, (gain_grads - gain_high.astype(full)).astype(low)])
    gain_parts = gain_parts.reshape((8, dp_count, part)).transpose((1, 0, 2)).reshape((dp_count, 8 * part))
    gain_width = -(-8 * part // (slot * LANE)) * LANE
    gain_parts = jnp.pad(gain_parts, ((0, 0), (0, slot * gain_width - 8 * part)))
    gain_parts = gain_parts.reshape((dp_count, slot, gain_width))
    home_grad = lax.all_to_all(
        jnp.concatenate([homeward(input_grad.astype(low)), gain_parts], axis=2),
        "dp", split_axis=0, concat_axis=0, tiled=True,
    )
    final_grad = landed(home_grad[:, :, :model_width])
    gain_sums = jnp.sum(
        home_grad[:, :, model_width:].reshape((dp_count, slot * gain_width))[:, : 8 * part].astype(full), axis=0
    )
    gain_sums = gain_sums.reshape((2, 4, part))
    gain_sums = gain_sums[0] + gain_sums[1]
    sizes = [select_rows, R, K, 1, 1, N, 1]
    cut_at = [sum(sizes[:k]) for k in range(len(sizes) + 1)]
    pieces = [small_sums[cut_at[k] : cut_at[k + 1]] for k in range(len(sizes))]
    return (
        final_out, final_grad, gain_sums[0], grad_w_in, pieces[2], pieces[3][0], pieces[0].T, pieces[1],
        pieces[4][0], pieces[5], pieces[6][0], grad_w_out, gain_sums[1], grad_one_in, grad_one_out,
        gain_sums[2], grad_w_qkv, grad_w_o, gain_sums[3], grad_two_in, grad_two_out,
    )


def solution(mesh):
    return jax.shard_map(
        shards,
        mesh=mesh,
        in_specs=(
            P("dp", None),
            P("dp", None),
            P("dp", None),
            P("dp", None),
            P("dp", None),
            P("dp"),
            P(None, None, ("dp", "tensor")),
            P(None, ("dp", "tensor")),
            P(("dp", "tensor")),
            P(("dp", "tensor"), None),
            P(None, ("dp", "tensor")),
            P(("dp", "tensor")),
            P(None, ("dp", "tensor")),
            P(("dp", "tensor")),
            P(("dp", "tensor"), None),
            P("dp"),
            P("dp", None, "tensor"),
            P("tensor", "dp"),
            P("dp"),
            P("dp", None, "tensor"),
            P("tensor", "dp"),
            P("dp"),
            P("dp", None, "tensor"),
            P("tensor", "dp"),
        ),
        out_specs=(
            P("dp", None),
            P("dp", None),
            P("dp"),
            P(None, None, ("dp", "tensor")),
            P(None, ("dp", "tensor")),
            P(("dp", "tensor")),
            P(("dp", "tensor"), None),
            P(None, ("dp", "tensor")),
            P(("dp", "tensor")),
            P(None, ("dp", "tensor")),
            P(("dp", "tensor")),
            P(("dp", "tensor"), None),
            P("dp"),
            P("dp", None, "tensor"),
            P("tensor", "dp"),
            P("dp"),
            P("dp", None, "tensor"),
            P("tensor", "dp"),
            P("dp"),
            P("dp", None, "tensor"),
            P("tensor", "dp"),
        ),
        check_vma=False,
    )
```
